32 devices in a mesh: ctx: 8 (over y, x, core), fsdp: 4 (over z).
Axes of the slice: x: 2, y: 2, z: 4, core: 2. Of those that a mesh axis runs over, the one named last changes fastest.
Arguments:
- hidden: bfloat16 [8, 2, 4, 64, 1024], P('ctx', None, 'fsdp'), may hold values from -6 to 6
- block_order: int32 [8, 2], replicated, may hold values from 0 to 15, as said below
- alibi_slopes: float32 [16], replicated, may hold values from 6.1035156e-05 to 0.05
- ln1_gain: bfloat16 [1024], P('fsdp'), may hold values from 0.25 to 1.75
- ln1_bias: bfloat16 [1024], P('fsdp'), may hold values from -4 to 4
- w_qkv: bfloat16 [1024, 3072], P('fsdp'), may hold values from -0.1875 to 0.1875
- qv_bias: bfloat16 [16, 128], P('fsdp'), may hold values from -4 to 4
- w_out: bfloat16 [1024, 1024], P('fsdp'), may hold values from -2 to 2
- out_bias: bfloat16 [1024], P('fsdp'), may hold values from -4 to 4
- ln2_gain: bfloat16 [1024], P('fsdp'), may hold values from 0.25 to 1.75
- ln2_bias: bfloat16 [1024], P('fsdp'), may hold values from -4 to 4
- w_up: bfloat16 [1024, 4096], P('fsdp'), may hold values from -0.1875 to 0.1875
- up_bias: bfloat16 [4096], P('fsdp'), may hold values from -4 to 4
- w_down: bfloat16 [4096, 1024], P('fsdp'), may hold values from -0.09375 to 0.09375
- down_bias: bfloat16 [1024], P('fsdp'), may hold values from -4 to 4
- d_output: bfloat16 [8, 2, 4, 64, 1024], P('ctx', None, 'fsdp'), may hold values from -6 to 6
Outputs:
- output: bfloat16 [8, 2, 4, 64, 1024], P('ctx', None, 'fsdp')
- d_hidden: bfloat16 [8, 2, 4, 64, 1024], P('ctx', None, 'fsdp')
- d_ln1_gain: float32 [1024], P('fsdp')
- d_ln1_bias: float32 [1024], P('fsdp')
- d_w_qkv: float32 [1024, 3072], P('fsdp')
- d_qv_bias: float32 [16, 128], P('fsdp')
- d_w_out: float32 [1024, 1024], P('fsdp')
- d_out_bias: float32 [1024], P('fsdp')
- d_ln2_gain: float32 [1024], P('fsdp')
- d_ln2_bias: float32 [1024], P('fsdp')
- d_w_up: float32 [1024, 4096], P('fsdp')
- d_up_bias: float32 [4096], P('fsdp')
- d_w_down: float32 [4096, 1024], P('fsdp')
- d_down_bias: float32 [1024], P('fsdp')
The draws below stay inside these ranges and needn't reach their ends.
Inputs may be any that keep to these rules, and one draw needn't show every extreme that they name: block_order names every block 0 to 15 once, and each row holds two blocks whose numbers add up to 15.
All inputs are finite; a program needn't handle non-finite values.
Results may differ from the reference program's by a relative error of at most 0.038.
Values may be sent and summed in bfloat16 or wider, within the bound.
A program may use at most 192 MiB of HBM per device.

```python
import math
import jax
import jax.numpy as jnp
from jax import lax

D = 1024
H = 16
HD = 64
FF = 4096
HALF = 64
N_CTX = 8
N_FSDP = 4


def draw_block_order(key, part):
    key = jax.random.fold_in(key, 7)
    chosen = jax.random.permutation(jax.random.fold_in(key, 1), N_CTX).astype(jnp.int32)
    flipped = jax.random.randint(jax.random.fold_in(key, 2), (N_CTX,), 0, 2).astype(jnp.int32)
    mirror = (2 * N_CTX - 1 - chosen).astype(jnp.int32)
    first_slot = jnp.where(flipped == 1, mirror, chosen)
    second_slot = jnp.where(flipped == 1, chosen, mirror)
    return jnp.stack([first_slot, second_slot], axis=1).astype(jnp.int32)


def block_scale(own_key, dims, cuts, least, largest):
    level = 1.0
    for position, parts in cuts:
        heights = jax.random.uniform(jax.random.fold_in(jax.random.fold_in(own_key, 6), position), (parts,), jnp.float32, least / len(cuts), largest / len(cuts))
        level = level * jnp.repeat(jnp.exp(heights), dims[position] // parts).reshape((-1,) + (1,) * (len(dims) - 1 - position))
    return level


def noise(rng, extent, deviation, most, cuts=(), held_as=jnp.bfloat16):
    values = jax.random.normal(rng, extent, jnp.float32) * deviation
    if len(cuts) > 0:
        values = block_scale(rng, extent, cuts, -0.22, 0.18) * values
    return jnp.clip(values, min=-most, max=most).astype(held_as)


def setup_inputs(seed: int = 0) -> dict:
    splits = jax.random.split(jax.random.key(seed), 17)
    hidden = noise(splits[0], (N_CTX, 2, N_FSDP, HALF, D), 1.0, 6.0, ((0, 8), (2, 4)))
    block_order = draw_block_order(jax.random.fold_in(splits[16], 71), 0)
    alibi_slopes = jnp.clip(jnp.exp(jax.random.uniform(splits[2], (H,), jnp.float32, math.log(6.103515625e-05), math.log(0.05))), 6.103515625e-05, 0.05)
    ln1_gain = jnp.clip(1.0 + 0.15 * jax.random.normal(splits[3], (D,), jnp.float32), 0.25, 1.75).astype(jnp.bfloat16)
    ln1_bias = noise(splits[4], (D,), 0.3, 4.0, ((0, 4),))
    w_qkv = noise(splits[5], (D, 3 * D), D ** -0.5, 0.1875, ((0, 4),))
    qv_bias = noise(splits[6], (H, 2 * HD), 0.3, 4.0, ((0, 4),))
    w_out = noise(splits[7], (D, D), 8 ** -0.5, 2.0, ((0, 4),))
    out_bias = noise(splits[8], (D,), 0.3, 4.0, ((0, 4),))
    ln2_gain = jnp.clip(1.0 + 0.15 * jax.random.normal(splits[9], (D,), jnp.float32), 0.25, 1.75).astype(jnp.bfloat16)
    ln2_bias = noise(splits[10], (D,), 0.3, 4.0, ((0, 4),))
    w_up = noise(splits[11], (D, FF), D ** -0.5, 0.1875, ((0, 4),))
    up_bias = noise(splits[12], (FF,), 0.3, 4.0, ((0, 4),))
    w_down = noise(splits[13], (FF, D), FF ** -0.5, 0.09375, ((0, 4),))
    down_bias = noise(splits[14], (D,), 0.3, 4.0, ((0, 4),))
    d_output = noise(splits[15], (N_CTX, 2, N_FSDP, HALF, D), 1.0, 6.0, ((0, 8), (2, 4)))
    return {"hidden": hidden, "block_order": block_order, "alibi_slopes": alibi_slopes, "ln1_gain": ln1_gain, "ln1_bias": ln1_bias, "w_qkv": w_qkv, "qv_bias": qv_bias, "w_out": w_out, "out_bias": out_bias, "ln2_gain": ln2_gain, "ln2_bias": ln2_bias, "w_up": w_up, "up_bias": up_bias, "w_down": w_down, "down_bias": down_bias, "d_output": d_output}


@jax.custom_vjp
def low(v):
    return lax.optimization_barrier(v.astype(jnp.bfloat16)).astype(jnp.float32)

@jax.custom_vjp
def low_back(v):
    return v

def low_keep(v):
    return (low(v), None)

def low_pass(kept, grad):
    return (grad,)

def back_keep(v):
    return (v, None)

def back_low(kept, grad):
    return (low(grad),)
low.defvjp(low_keep, low_pass)
low_back.defvjp(back_keep, back_low)
HIGHEST = lax.Precision.HIGHEST
NEGATIVE = -1e+30
EPSILON = 1e-05
TANH_SCALE = 0.7978845608028654

def matmul(left, right):
    return jnp.dot(left, right, precision=HIGHEST, preferred_element_type=jnp.float32)

def norm_forward(rows_in, gain, shift):
    centred = rows_in - lax.optimization_barrier(jnp.mean(rows_in, axis=-1, keepdims=True))
    inv_std = lax.rsqrt(lax.optimization_barrier(jnp.mean(centred * centred, axis=-1, keepdims=True)) + EPSILON)
    return centred * inv_std * gain + shift

def gelu_tanh(values):
    return 0.5 * values * (1.0 + jnp.tanh(TANH_SCALE * (values + 0.044715 * values * values * values)))

def token_positions(block_order):
    block_start = block_order.astype(jnp.int32)[:, :, None, None] * (N_FSDP * HALF)
    inner_pos = (jnp.arange(N_FSDP, dtype=jnp.int32) * HALF)[None, None, :, None] + jnp.arange(HALF, dtype=jnp.int32)[None, None, None, :]
    return (block_start + inner_pos).reshape(-1).astype(jnp.int32)

def attention(queries, keys, values, positions, slopes):
    length = queries.shape[0]
    q_block = min(512, length)
    n_blocks = length // q_block

    def query_block(inputs):
        query_rows, query_pos = inputs
        raw_score = jnp.einsum('qhd,khd->hqk', query_rows, keys, precision=HIGHEST) * (1.0 / math.sqrt(HD))
        pos_gap = (query_pos[:, None] - positions[None, :]).astype(jnp.float32)
        raw_score = low_back(raw_score - slopes[:, None, None] * pos_gap[None])
        allowed = (positions[None, :] <= query_pos[:, None])[None]
        raw_score = jnp.where(allowed, raw_score, NEGATIVE)
        row_max = lax.optimization_barrier(jnp.max(raw_score, axis=-1, keepdims=True))
        exp_terms = jnp.exp(raw_score - row_max)
        soft_probs = exp_terms / lax.optimization_barrier(jnp.sum(exp_terms, axis=-1, keepdims=True))
        return jnp.einsum('hqk,khd->qhd', low(soft_probs), values, precision=HIGHEST)
    blocks_out = lax.map(jax.checkpoint(query_block), (queries.reshape(n_blocks, q_block, H, HD), positions.reshape(n_blocks, q_block)))
    return blocks_out.reshape(length, H * HD)

def layer_forward(rows_in, ln1_gain, ln1_bias, w_qkv, qv_bias, w_out, out_bias, ln2_gain, ln2_bias, w_up, up_bias, w_down, down_bias, positions, slopes):
    first_in = low(norm_forward(rows_in, ln1_gain, ln1_bias))
    zero_bias = jnp.zeros((H, HD), jnp.float32)
    joined_bias = jnp.concatenate([qv_bias[:, :HD], zero_bias, qv_bias[:, HD:]], axis=1).reshape(3 * D)
    joined = low_back(low(matmul(first_in, w_qkv) + joined_bias)).reshape(-1, H, 3, HD)
    attended = low_back(low(attention(joined[:, :, 0], joined[:, :, 1], joined[:, :, 2], positions, slopes)))
    middle = rows_in + low_back(matmul(attended, w_out) + out_bias)
    second_in = low(norm_forward(middle, ln2_gain, ln2_bias))
    hidden_pre = low_back(matmul(second_in, w_up) + up_bias)
    activated = low_back(low(gelu_tanh(hidden_pre)))
    return middle + low_back(matmul(activated, w_down) + down_bias)

def reference(hidden, block_order, alibi_slopes, ln1_gain, ln1_bias, w_qkv, qv_bias, w_out, out_bias, ln2_gain, ln2_bias, w_up, up_bias, w_down, down_bias, d_output):
    positions = token_positions(block_order)
    rows_in = hidden.astype(jnp.float32).reshape(-1, D)
    weights = tuple((param.astype(jnp.float32) for param in (ln1_gain, ln1_bias, w_qkv, qv_bias, w_out, out_bias, ln2_gain, ln2_bias, w_up, up_bias, w_down, down_bias)))

    def forward(rows_now, *params):
        return layer_forward(rows_now, *params, positions, alibi_slopes)
    result, pull_back = jax.vjp(forward, rows_in, *weights)
    grads = pull_back(d_output.astype(jnp.float32).reshape(-1, D))
    output = result.astype(jnp.bfloat16).reshape(hidden.shape)
    d_hidden = grads[0].astype(jnp.bfloat16).reshape(hidden.shape)
    return (output, d_hidden, grads[1], grads[2], grads[3], grads[4], grads[5], grads[6], grads[7], grads[8], grads[9], grads[10], grads[11], grads[12])
```

```python
import functools

import jax
import jax.numpy as jnp
from jax import lax
from jax.experimental import pallas as pl
from jax.experimental.pallas import tpu as pltpu
from jax.sharding import PartitionSpec as P

EPSILON = 1e-05
NEGATIVE = -1e30
TANH_SCALE = 0.7978845608028654


def gelu_tanh(values):
    return (
        0.5 * values * (1.0 + jnp.tanh(TANH_SCALE * (values + 0.044715 * values * values * values)))
    )


def norm_parts(rows_in):
    centred = rows_in - jnp.mean(rows_in, axis=-1, keepdims=True)
    inv_std = lax.rsqrt(jnp.mean(centred * centred, axis=-1, keepdims=True) + EPSILON)
    return (centred * inv_std, inv_std)


def norm_back(d_norm, gain, normed, inv_std):
    scaled = d_norm * gain
    return inv_std * (
        scaled
        - jnp.mean(scaled, axis=-1, keepdims=True)
        - normed * jnp.mean(scaled * normed, axis=-1, keepdims=True)
    )


TILE_BLOCKS = 4


def dot_nt(left, right):
    return lax.dot_general(left, right, (((1,), (1,)), ((), ())), preferred_element_type=jnp.float32)


def dot_nn(left, right):
    return jnp.dot(left, right, preferred_element_type=jnp.float32)


def query_places(tile, part, query_rows, tile_rows, block_span):
    lane = lax.broadcasted_iota(jnp.int32, (1, tile_rows), 1)
    block = tile * TILE_BLOCKS + lane // query_rows
    return (block * block_span + part * query_rows + lane % query_rows).astype(jnp.float32)


def key_places(block, block_span):
    row = lax.broadcasted_iota(jnp.int32, (block_span, 1), 0)
    return (block * block_span + row).astype(jnp.float32)


def sort_rows(slots, source, first, half, width, target, scale):
    blocks = source.shape[0]

    def step(block, carry):
        packed = source[slots[block], pl.ds(first, half), :].astype(jnp.float32) * scale
        base = pl.multiple_of(block * 2 * half, 2 * half)
        target[pl.ds(base, half), :] = packed[:, :width].astype(target.dtype)
        target[pl.ds(base + half, half), :] = packed[:, width:].astype(target.dtype)
        return carry

    lax.fori_loop(0, blocks, step, 0)


def unsort_rows(slots, source, first, half, target):
    blocks = target.shape[0]

    def step(block, carry):
        base = pl.multiple_of(block * 2 * half, 2 * half)
        packed = jnp.concatenate(
            [source[pl.ds(base, half), :], source[pl.ds(base + half, half), :]], axis=1
        )
        target[slots[block], pl.ds(first, half), :] = packed.astype(target.dtype)
        return carry

    lax.fori_loop(0, blocks, step, 0)


def attend_kernel(
    block_span, slots, part, slope, packed, out, out_t, lse, sorted_q, run_max, run_sum, sorted_o
):
    blocks = packed.shape[0]
    half = packed.shape[1] - block_span
    width = packed.shape[2] // 2
    rows = 2 * half
    tile_rows = TILE_BLOCKS * rows
    sort_rows(slots, packed, block_span, half, width, sorted_q, 0.125)
    run_max[...] = jnp.full_like(run_max, NEGATIVE)
    run_sum[...] = jnp.zeros_like(run_sum)
    out_t[...] = jnp.zeros_like(out_t)
    slope_now = slope[0]
    part_now = part[0]

    def key_step(block, carry):
        keys = packed[slots[block], pl.ds(0, block_span), :]
        values_t = keys[:, width:].astype(jnp.float32).T.astype(jnp.bfloat16)
        keys = keys[:, :width]
        key_pos = key_places(block, block_span)

        def tile_step(tile, inner):
            base = pl.multiple_of(tile * tile_rows, tile_rows)
            where = pl.ds(base, tile_rows)
            gap = query_places(tile, part_now, rows, tile_rows, block_span) - key_pos
            score = dot_nt(keys, sorted_q[where, :]) - slope_now * gap
            score = jnp.where(gap >= 0.0, score, NEGATIVE)
            old_max = run_max[:, where]
            new_max = jnp.maximum(old_max, jnp.max(score, axis=0, keepdims=True))
            weights = jnp.exp(score - new_max)
            shrink = jnp.exp(old_max - new_max)
            run_max[:, where] = new_max
            run_sum[:, where] = run_sum[:, where] * shrink + jnp.sum(
                weights, axis=0, keepdims=True
            )
            out_t[:, where] = out_t[:, where] * shrink + dot_nn(
                values_t, weights.astype(jnp.bfloat16)
            )
            return inner

        lax.fori_loop(block // TILE_BLOCKS, blocks // TILE_BLOCKS, tile_step, 0)
        return carry

    lax.fori_loop(0, blocks, key_step, 0)
    out_t[...] = out_t[...] / run_sum[...]
    lse[...] = run_max[...] + jnp.log(run_sum[...])
    sorted_o[...] = out_t[...].T
    unsort_rows(slots, sorted_o, 0, half, out)


def attend_back_kernel(
    block_span,
    slots,
    part,
    slope,
    packed,
    grad_out,
    out_t,
    lse,
    grads,
    sorted_q,
    sorted_g,
    delta,
    grad_q_t,
    sorted_dq,
):
    blocks = packed.shape[0]
    half = packed.shape[1] - block_span
    width = packed.shape[2] // 2
    rows = 2 * half
    tile_rows = TILE_BLOCKS * rows
    sort_rows(slots, packed, block_span, half, width, sorted_q, 0.125)
    sort_rows(slots, grad_out, 0, half, width, sorted_g, 1.0)
    delta[...] = jnp.sum(
        sorted_g[...].astype(jnp.float32).T * out_t[...], axis=0, keepdims=True
    )
    grad_q_t[...] = jnp.zeros_like(grad_q_t)
    slope_now = slope[0]
    part_now = part[0]

    def key_step(block, carry):
        keys = packed[slots[block], pl.ds(0, block_span), :]
        values = keys[:, width:]
        keys = keys[:, :width]
        keys_t = keys.astype(jnp.float32).T.astype(jnp.bfloat16)
        key_pos = key_places(block, block_span)

        def tile_step(tile, sums):
            grad_k, grad_v = sums
            base = pl.multiple_of(tile * tile_rows, tile_rows)
            where = pl.ds(base, tile_rows)
            query_now = sorted_q[where, :]
            grad_now = sorted_g[where, :]
            gap = query_places(tile, part_now, rows, tile_rows, block_span) - key_pos
            score = dot_nt(keys, query_now) - slope_now * gap
            score = jnp.where(gap >= 0.0, score, NEGATIVE)
            probs = jnp.exp(score - lse[:, where])
            grad_v = grad_v + dot_nn(probs.astype(jnp.bfloat16), grad_now)
            grad_score = probs * (dot_nt(values, grad_now) - delta[:, where])
            grad_score = grad_score.astype(jnp.bfloat16)
            grad_k = grad_k + dot_nn(grad_score, query_now)
            grad_q_t[:, where] = grad_q_t[:, where] + dot_nn(keys_t, grad_score)
            return (grad_k, grad_v)

        zero = jnp.zeros((block_span, width), jnp.float32)
        grad_k, grad_v = lax.fori_loop(
            block // TILE_BLOCKS, blocks // TILE_BLOCKS, tile_step, (zero, zero)
        )
        grads[slots[block], pl.ds(0, block_span), :] = jnp.concatenate(
            [grad_k, grad_v], axis=1
        ).astype(grads.dtype)
        return carry

    lax.fori_loop(0, blocks, key_step, 0)
    sorted_dq[...] = grad_q_t[...].T * 0.125
    unsort_rows(slots, sorted_dq, block_span, half, grads)


def smem():
    return pl.BlockSpec(memory_space=pltpu.SMEM)


def vmem():
    return pl.BlockSpec(memory_space=pltpu.VMEM)


def attend(slots, part, slope, packed, block_span):
    blocks, packed_rows, lanes = packed.shape
    half = packed_rows - block_span
    width = lanes // 2
    total = blocks * 2 * half
    return pl.pallas_call(
        functools.partial(attend_kernel, block_span),
        out_shape=(
            jax.ShapeDtypeStruct((blocks, half, lanes), jnp.bfloat16),
            jax.ShapeDtypeStruct((width, total), jnp.float32),
            jax.ShapeDtypeStruct((1, total), jnp.float32),
        ),
        in_specs=[smem(), smem(), smem(), vmem()],
        out_specs=(vmem(), vmem(), vmem()),
        scratch_shapes=[
            pltpu.VMEM((total, width), jnp.bfloat16),
            pltpu.VMEM((1, total), jnp.float32),
            pltpu.VMEM((1, total), jnp.float32),
            pltpu.VMEM((total, width), jnp.float32),
        ],
        compiler_params=pltpu.CompilerParams(vmem_limit_bytes=48 * 1024 * 1024),
        cost_estimate=pl.CostEstimate(
            flops=2 * total * blocks * block_span * lanes,
            bytes_accessed=4 * packed.size,
            transcendentals=total * blocks * block_span // 2,
        ),
        name="attend",
    )(slots, part, slope, packed)


def attend_back(slots, part, slope, packed, grad_out, out_t, lse, block_span):
    blocks, packed_rows, lanes = packed.shape
    half = packed_rows - block_span
    width = lanes // 2
    total = blocks * 2 * half
    return pl.pallas_call(
        functools.partial(attend_back_kernel, block_span),
        out_shape=jax.ShapeDtypeStruct(packed.shape, jnp.bfloat16),
        in_specs=[smem(), smem(), smem(), vmem(), vmem(), vmem(), vmem()],
        out_specs=vmem(),
        scratch_shapes=[
            pltpu.VMEM((total, width), jnp.bfloat16),
            pltpu.VMEM((total, width), jnp.bfloat16),
            pltpu.VMEM((1, total), jnp.float32),
            pltpu.VMEM((width, total), jnp.float32),
            pltpu.VMEM((total, width), jnp.float32),
        ],
        compiler_params=pltpu.CompilerParams(vmem_limit_bytes=48 * 1024 * 1024),
        cost_estimate=pl.CostEstimate(
            flops=5 * total * blocks * block_span * width,
            bytes_accessed=8 * packed.size,
            transcendentals=total * blocks * block_span // 2,
        ),
        name="attend_back",
    )(slots, part, slope, packed, grad_out, out_t, lse)


def local(
    hidden,
    block_order,
    alibi_slopes,
    ln1_gain,
    ln1_bias,
    w_qkv,
    qv_bias,
    w_out,
    out_bias,
    ln2_gain,
    ln2_bias,
    w_up,
    up_bias,
    w_down,
    down_bias,
    d_output,
):
    f32 = jnp.float32
    b16 = jnp.bfloat16
    half_rows = hidden.shape[3]
    width = hidden.shape[4]
    tok_rows = 2 * half_rows
    groups = lax.axis_size("fsdp")
    ctx_size = lax.axis_size("ctx")
    head_count = alibi_slopes.shape[0]
    head_width = width // head_count
    heads = head_count // groups
    span = tok_rows * groups
    block_span = half_rows * groups
    parts = ctx_size // heads
    part_groups = groups // parts
    query_rows = part_groups * half_rows
    half = query_rows // 2
    qkv_cols = 3 * width // groups
    up_cols = w_up.shape[1] // groups
    ctx_index = lax.axis_index("ctx")
    group_index = lax.axis_index("fsdp")
    shard = width // groups

    def gather(rows, axis_name):
        return lax.all_gather(rows, axis_name, axis=0, tiled=True)

    def exchange(rows, axis_name):
        return lax.all_to_all(rows, axis_name, split_axis=0, concat_axis=0, tiled=True)

    def scatter(rows):
        return lax.psum_scatter(
            rows.astype(b16), "fsdp", scatter_dimension=0, tiled=True
        ).astype(f32)

    cut = w_qkv.shape[0] // ctx_size
    cut_qkv = lax.dynamic_slice_in_dim(w_qkv, ctx_index * cut, cut).reshape(cut, groups, qkv_cols)
    cut_up = lax.dynamic_slice_in_dim(w_up, ctx_index * cut, cut).reshape(cut, groups, up_cols)
    cut_both = exchange(
        jnp.concatenate([cut_qkv, cut_up], axis=2).transpose(1, 0, 2), "fsdp"
    )

    def own_columns(cut_cols):
        whole = lax.all_gather(cut_cols, "ctx", axis=0)
        return whole.transpose(1, 0, 2, 3).reshape(width, cut_cols.shape[2])

    own_qkv = own_columns(cut_both[:, :, :qkv_cols])
    own_up = own_columns(cut_both[:, :, qkv_cols:])

    own_rows = hidden.reshape(tok_rows, width)
    grad_out = d_output.reshape(tok_rows, width)
    small = jnp.stack([ln1_gain, ln1_bias, out_bias, ln2_gain, ln2_bias, down_bias])
    small = jnp.pad(small, ((0, 10), (0, width - shard)))
    with_small = gather(jnp.concatenate([own_rows, small], axis=0), "fsdp").reshape(
        groups, tok_rows + 16, width
    )
    full_small = (
        with_small[:, tok_rows : tok_rows + 6, :shard].transpose(1, 0, 2).reshape(6, width)
    ).astype(f32)
    full_g1, full_b1, full_bo, full_g2, full_b2, full_bd = (full_small[i] for i in range(6))
    all_rows = with_small[:, :tok_rows].reshape(span, width)
    all_grad = gather(grad_out, "fsdp")

    rows_in = own_rows.astype(f32)
    normed_one, inv_one = norm_parts(rows_in)
    first_in = (norm_parts(all_rows.astype(f32))[0] * full_g1 + full_b1).astype(b16)
    joined_bias = jnp.concatenate(
        [
            qv_bias[:, :head_width],
            jnp.zeros((heads, head_width), b16),
            qv_bias[:, head_width:],
        ],
        axis=1,
    ).reshape(qkv_cols)
    joined = (dot_nn(first_in, own_qkv) + joined_bias.astype(f32)).astype(b16)

    joined = joined.reshape(parts, part_groups, 2, half_rows, heads, 3 * head_width)

    def pack_queries(rows):
        rows = rows.transpose(4, 0, 2, 1, 3, 5).reshape(
            ctx_size, 2, 2, half, head_width
        )
        return jnp.concatenate([rows[:, :, 0], rows[:, :, 1]], axis=-1)

    def unpack_queries(rows):
        rows = jnp.stack([rows[..., :head_width], rows[..., head_width:]], axis=2)
        return rows.reshape(
            heads, parts, 2, part_groups, half_rows, head_width
        ).transpose(1, 3, 2, 4, 0, 5)

    keys_values = (
        joined[..., head_width:]
        .transpose(4, 2, 0, 1, 3, 5)
        .reshape(heads, 1, 2, block_span, 2 * head_width)
    )
    keys_values = jnp.broadcast_to(
        keys_values, (heads, parts, 2, block_span, 2 * head_width)
    ).reshape(ctx_size, 2, block_span, 2 * head_width)
    packed = exchange(
        jnp.concatenate([keys_values, pack_queries(joined[..., :head_width])], axis=2), "ctx"
    ).reshape(2 * ctx_size, block_span + half, 2 * head_width)

    flat_order = block_order.reshape(-1)
    slot_ids = jnp.arange(2 * ctx_size, dtype=jnp.int32)
    slots = jnp.sum(
        jnp.where(flat_order[None, :] == slot_ids[:, None], slot_ids[None, :], 0), axis=1
    ).astype(jnp.int32)
    part = (ctx_index % parts).astype(jnp.int32).reshape(1)
    slope = lax.dynamic_slice_in_dim(alibi_slopes, group_index * heads + ctx_index // parts, 1)
    out_packed, out_t, lse = attend(slots, part, slope, packed, block_span)

    attended = unpack_queries(
        exchange(out_packed.reshape(ctx_size, 2, half, 2 * head_width), "ctx")
    ).reshape(span, heads * head_width)
    middle = rows_in + scatter(dot_nn(attended, w_out)) + full_bo
    normed_two, inv_two = norm_parts(middle)
    second_in = gather((normed_two * full_g2 + full_b2).astype(b16), "fsdp")
    hidden_pre = dot_nn(second_in, own_up) + up_bias.astype(f32)
    activated, gelu_pull = jax.vjp(gelu_tanh, hidden_pre)
    activated = activated.astype(b16)
    result = middle + scatter(dot_nn(activated, w_down)) + full_bd
    output = result.astype(b16).reshape(hidden.shape)

    grad_act = dot_nt(all_grad, w_down).astype(b16)
    grad_pre = gelu_pull(grad_act.astype(f32))[0].astype(b16)
    grad_second = scatter(dot_nt(grad_pre, own_up))
    grad_middle = grad_out.astype(f32) + norm_back(grad_second, full_g2, normed_two, inv_two)
    grad_branch = gather(grad_middle.astype(b16), "fsdp")
    grad_attended = dot_nt(grad_branch, w_out).astype(b16)
    grad_packed = exchange(
        pack_queries(
            grad_attended.reshape(parts, part_groups, 2, half_rows, heads, head_width)
        ),
        "ctx",
    ).reshape(2 * ctx_size, half, 2 * head_width)
    grads = attend_back(slots, part, slope, packed, grad_packed, out_t, lse, block_span)
    grads = exchange(
        grads.reshape(ctx_size, 2, block_span + half, 2 * head_width), "ctx"
    )
    grad_q = unpack_queries(grads[:, :, block_span:]).reshape(span, heads, head_width)
    grad_kv = jnp.sum(
        grads[:, :, :block_span]
        .reshape(heads, parts, 2, groups, half_rows, 2 * head_width)
        .astype(f32),
        axis=1,
    ).astype(b16)
    grad_kv = grad_kv.transpose(2, 1, 3, 0, 4).reshape(span, heads, 2 * head_width)
    grad_joined = jnp.concatenate([grad_q, grad_kv], axis=2).reshape(span, qkv_cols)
    grad_first = scatter(dot_nt(grad_joined, own_qkv))
    grad_rows = grad_middle + norm_back(grad_first, full_g1, normed_one, inv_one)
    d_hidden = grad_rows.astype(b16).reshape(hidden.shape)

    def dot_tn(left, right):
        return lax.dot_general(
            left, right, (((0,), (0,)), ((), ())), preferred_element_type=f32
        ).astype(b16)

    def own_row_sums(cols):
        cols = cols.reshape(groups, ctx_size, cut, cols.shape[1]).transpose(1, 0, 2, 3)
        summed = lax.psum_scatter(cols, "ctx", scatter_dimension=0, tiled=True)
        moved = exchange(summed[0], "fsdp").transpose(1, 0, 2)
        return gather(moved.reshape(cut, -1), "ctx").astype(f32)

    d_w_down, d_w_out = lax.psum(
        (dot_tn(activated, all_grad), dot_tn(attended, grad_branch)), "ctx"
    )
    d_w_up = own_row_sums(dot_tn(second_in, grad_pre))
    d_w_qkv = own_row_sums(dot_tn(first_in, grad_joined))

    def own_sum(rows):
        return lax.dynamic_slice_in_dim(
            jnp.sum(rows.astype(f32), axis=0), group_index * shard, shard
        )

    joined_sums = jnp.sum(grad_joined.astype(f32), axis=0).reshape(heads, 3, head_width)
    sum_qv = jnp.concatenate([joined_sums[:, 0], joined_sums[:, 2]], axis=1)
    early = lax.psum(
        jnp.concatenate(
            [
                jnp.sum(grad_pre.astype(f32), axis=0),
                own_sum(grad_branch),
                own_sum(all_grad),
            ]
        ),
        "ctx",
    )
    d_up_bias = early[:up_cols]
    d_out_bias = early[up_cols : up_cols + shard]
    d_down_bias = early[up_cols + shard :]
    spread = jnp.where(
        jnp.arange(groups)[:, None] == group_index, sum_qv.reshape(1, -1), 0.0
    ).reshape(-1)
    late = lax.psum(
        jnp.concatenate(
            [
                jnp.sum(grad_first * normed_one, axis=0),
                jnp.sum(grad_first, axis=0),
                jnp.sum(grad_second * normed_two, axis=0),
                jnp.sum(grad_second, axis=0),
                spread,
            ]
        ),
        ("ctx", "fsdp"),
    )
    norm_sums = late[: 4 * width].reshape(4, groups, shard)
    norm_sums = lax.dynamic_slice_in_dim(norm_sums, group_index, 1, axis=1)[:, 0]
    d_qv_bias = lax.dynamic_slice_in_dim(
        late[4 * width :].reshape((groups,) + sum_qv.shape), group_index, 1
    )[0]
    return (
        output,
        d_hidden,
        norm_sums[0],
        norm_sums[1],
        d_w_qkv,
        d_qv_bias,
        d_w_out.astype(f32),
        d_out_bias,
        norm_sums[2],
        norm_sums[3],
        d_w_up,
        d_up_bias,
        d_w_down.astype(f32),
        d_down_bias,
    )


def solution(mesh):
    placed = (
        P("ctx", None, "fsdp", None, None),
        P(),
        P(),
        P("fsdp"),
        P("fsdp"),
        P("fsdp", None),
        P("fsdp", None),
        P("fsdp", None),
        P("fsdp"),
        P("fsdp"),
        P("fsdp"),
        P("fsdp", None),
        P("fsdp"),
        P("fsdp", None),
        P("fsdp"),
        P("ctx", None, "fsdp", None, None),
    )
    return jax.shard_map(
        local,
        mesh=mesh,
        in_specs=placed,
        out_specs=(
            P("ctx", None, "fsdp", None, None),
            P("ctx", None, "fsdp", None, None),
            P("fsdp"),
            P("fsdp"),
            P("fsdp", None),
            P("fsdp", None),
            P("fsdp", None),
            P("fsdp"),
            P("fsdp"),
            P("fsdp"),
            P("fsdp", None),
            P("fsdp"),
            P("fsdp", None),
            P("fsdp"),
        ),
        check_vma=False,
    )
```

```python
import functools

import jax
import jax.numpy as jnp
from jax import lax
from jax.experimental import pallas as pl
from jax.experimental.pallas import tpu as pltpu
from jax.sharding import PartitionSpec as P

EPSILON = 1e-05
NEGATIVE = -1e30
TANH_SCALE = 0.7978845608028654


def gelu_tanh(values):
    return (
        0.5 * values * (1.0 + jnp.tanh(TANH_SCALE * (values + 0.044715 * values * values * values)))
    )


def norm_parts(rows_in):
    centred = rows_in - jnp.mean(rows_in, axis=-1, keepdims=True)
    inv_std = lax.rsqrt(jnp.mean(centred * centred, axis=-1, keepdims=True) + EPSILON)
    return (centred * inv_std, inv_std)


def norm_back(d_norm, gain, normed, inv_std):
    scaled = d_norm * gain
    return inv_std * (
        scaled
        - jnp.mean(scaled, axis=-1, keepdims=True)
        - normed * jnp.mean(scaled * normed, axis=-1, keepdims=True)
    )


TILE_BLOCKS = 4


def dot_nt(left, right):
    return lax.dot_general(left, right, (((1,), (1,)), ((), ())), preferred_element_type=jnp.float32)


def dot_nn(left, right):
    return jnp.dot(left, right, preferred_element_type=jnp.float32)


def query_places(tile, part, query_rows, tile_rows, block_span):
    lane = lax.broadcasted_iota(jnp.int32, (1, tile_rows), 1)
    block = tile * TILE_BLOCKS + lane // query_rows
    return (block * block_span + part * query_rows + lane % query_rows).astype(jnp.float32)


def key_places(block, block_span):
    row = lax.broadcasted_iota(jnp.int32, (block_span, 1), 0)
    return (block * block_span + row).astype(jnp.float32)


def sort_rows(slots, source, first, half, width, target, scale):
    blocks = source.shape[0]

    def step(block, carry):
        packed = source[slots[block], pl.ds(first, half), :].astype(jnp.float32) * scale
        base = pl.multiple_of(block * 2 * half, 2 * half)
        target[pl.ds(base, half), :] = packed[:, :width].astype(target.dtype)
        target[pl.ds(base + half, half), :] = packed[:, width:].astype(target.dtype)
        return carry

    lax.fori_loop(0, blocks, step, 0)


def unsort_rows(slots, source, first, half, target):
    blocks = target.shape[0]

    def step(block, carry):
        base = pl.multiple_of(block * 2 * half, 2 * half)
        packed = jnp.concatenate(
            [source[pl.ds(base, half), :], source[pl.ds(base + half, half), :]], axis=1
        )
        target[slots[block], pl.ds(first, half), :] = packed.astype(target.dtype)
        return carry

    lax.fori_loop(0, blocks, step, 0)


def attend_kernel(
    block_span, slots, part, slope, packed, out, out_t, lse, sorted_q, run_max, run_sum, sorted_o
):
    blocks = packed.shape[0]
    half = packed.shape[1] - block_span
    width = packed.shape[2] // 2
    rows = 2 * half
    tile_rows = TILE_BLOCKS * rows
    sort_rows(slots, packed, block_span, half, width, sorted_q, 0.125)
    run_max[...] = jnp.full_like(run_max, NEGATIVE)
    run_sum[...] = jnp.zeros_like(run_sum)
    out_t[...] = jnp.zeros_like(out_t)
    slope_now = slope[0]
    part_now = part[0]

    def key_step(block, carry):
        keys = packed[slots[block], pl.ds(0, block_span), :]
        values_t = keys[:, width:].astype(jnp.float32).T.astype(jnp.bfloat16)
        keys = keys[:, :width]
        key_pos = key_places(block, block_span)

        def tile_step(tile, inner):
            base = pl.multiple_of(tile * tile_rows, tile_rows)
            where = pl.ds(base, tile_rows)
            gap = query_places(tile, part_now, rows, tile_rows, block_span) - key_pos
            score = dot_nt(keys, sorted_q[where, :]) - slope_now * gap
            score = jnp.where(gap >= 0.0, score, NEGATIVE)
            old_max = run_max[:, where]
            new_max = jnp.maximum(old_max, jnp.max(score, axis=0, keepdims=True))
            weights = jnp.exp(score - new_max)
            shrink = jnp.exp(old_max - new_max)
            run_max[:, where] = new_max
            run_sum[:, where] = run_sum[:, where] * shrink + jnp.sum(
                weights, axis=0, keepdims=True
            )
            out_t[:, where] = out_t[:, where] * shrink + dot_nn(
                values_t, weights.astype(jnp.bfloat16)
            )
            return inner

        lax.fori_loop(block // TILE_BLOCKS, blocks // TILE_BLOCKS, tile_step, 0)
        return carry

    lax.fori_loop(0, blocks, key_step, 0)
    out_t[...] = out_t[...] / run_sum[...]
    lse[...] = run_max[...] + jnp.log(run_sum[...])
    sorted_o[...] = out_t[...].T
    unsort_rows(slots, sorted_o, 0, half, out)


def attend_back_kernel(
    block_span,
    slots,
    part,
    slope,
    packed,
    grad_out,
    out_t,
    lse,
    grads,
    sorted_q,
    sorted_g,
    delta,
    grad_q_t,
    sorted_dq,
):
    blocks = packed.shape[0]
    half = packed.shape[1] - block_span
    width = packed.shape[2] // 2
    rows = 2 * half
    tile_rows = TILE_BLOCKS * rows
    sort_rows(slots, packed, block_span, half, width, sorted_q, 0.125)
    sort_rows(slots, grad_out, 0, half, width, sorted_g, 1.0)
    delta[...] = jnp.sum(
        sorted_g[...].astype(jnp.float32).T * out_t[...], axis=0, keepdims=True
    )
    grad_q_t[...] = jnp.zeros_like(grad_q_t)
    slope_now = slope[0]
    part_now = part[0]

    def key_step(block, carry):
        keys = packed[slots[block], pl.ds(0, block_span), :]
        values = keys[:, width:]
        keys = keys[:, :width]
        keys_t = keys.astype(jnp.float32).T.astype(jnp.bfloat16)
        key_pos = key_places(block, block_span)

        def tile_step(tile, sums):
            grad_k, grad_v = sums
            base = pl.multiple_of(tile * tile_rows, tile_rows)
            where = pl.ds(base, tile_rows)
            query_now = sorted_q[where, :]
            grad_now = sorted_g[where, :]
            gap = query_places(tile, part_now, rows, tile_rows, block_span) - key_pos
            score = dot_nt(keys, query_now) - slope_now * gap
            score = jnp.where(gap >= 0.0, score, NEGATIVE)
            probs = jnp.exp(score - lse[:, where])
            grad_v = grad_v + dot_nn(probs.astype(jnp.bfloat16), grad_now)
            grad_score = probs * (dot_nt(values, grad_now) - delta[:, where])
            grad_score = grad_score.astype(jnp.bfloat16)
            grad_k = grad_k + dot_nn(grad_score, query_now)
            grad_q_t[:, where] = grad_q_t[:, where] + dot_nn(keys_t, grad_score)
            return (grad_k, grad_v)

        zero = jnp.zeros((block_span, width), jnp.float32)
        grad_k, grad_v = lax.fori_loop(
            block // TILE_BLOCKS, blocks // TILE_BLOCKS, tile_step, (zero, zero)
        )
        grads[slots[block], pl.ds(0, block_span), :] = jnp.concatenate(
            [grad_k, grad_v], axis=1
        ).astype(grads.dtype)
        return carry

    lax.fori_loop(0, blocks, key_step, 0)
    sorted_dq[...] = grad_q_t[...].T * 0.125
    unsort_rows(slots, sorted_dq, block_span, half, grads)


def smem():
    return pl.BlockSpec(memory_space=pltpu.SMEM)


def vmem():
    return pl.BlockSpec(memory_space=pltpu.VMEM)


def attend(slots, part, slope, packed, block_span):
    blocks, packed_rows, lanes = packed.shape
    half = packed_rows - block_span
    width = lanes // 2
    total = blocks * 2 * half
    return pl.pallas_call(
        functools.partial(attend_kernel, block_span),
        out_shape=(
            jax.ShapeDtypeStruct((blocks, half, lanes), jnp.bfloat16),
            jax.ShapeDtypeStruct((width, total), jnp.float32),
            jax.ShapeDtypeStruct((1, total), jnp.float32),
        ),
        in_specs=[smem(), smem(), smem(), vmem()],
        out_specs=(vmem(), vmem(), vmem()),
        scratch_shapes=[
            pltpu.VMEM((total, width), jnp.bfloat16),
            pltpu.VMEM((1, total), jnp.float32),
            pltpu.VMEM((1, total), jnp.float32),
            pltpu.VMEM((total, width), jnp.float32),
        ],
        compiler_params=pltpu.CompilerParams(vmem_limit_bytes=48 * 1024 * 1024),
        cost_estimate=pl.CostEstimate(
            flops=2 * total * blocks * block_span * lanes,
            bytes_accessed=4 * packed.size,
            transcendentals=total * blocks * block_span // 2,
        ),
        name="attend",
    )(slots, part, slope, packed)


def attend_back(slots, part, slope, packed, grad_out, out_t, lse, block_span):
    blocks, packed_rows, lanes = packed.shape
    half = packed_rows - block_span
    width = lanes // 2
    total = blocks * 2 * half
    return pl.pallas_call(
        functools.partial(attend_back_kernel, block_span),
        out_shape=jax.ShapeDtypeStruct(packed.shape, jnp.bfloat16),
        in_specs=[smem(), smem(), smem(), vmem(), vmem(), vmem(), vmem()],
        out_specs=vmem(),
        scratch_shapes=[
            pltpu.VMEM((total, width), jnp.bfloat16),
            pltpu.VMEM((total, width), jnp.bfloat16),
            pltpu.VMEM((1, total), jnp.float32),
            pltpu.VMEM((width, total), jnp.float32),
            pltpu.VMEM((total, width), jnp.float32),
        ],
        compiler_params=pltpu.CompilerParams(vmem_limit_bytes=48 * 1024 * 1024),
        cost_estimate=pl.CostEstimate(
            flops=5 * total * blocks * block_span * width,
            bytes_accessed=8 * packed.size,
            transcendentals=total * blocks * block_span // 2,
        ),
        name="attend_back",
    )(slots, part, slope, packed, grad_out, out_t, lse)


def local(
    hidden,
    block_order,
    alibi_slopes,
    ln1_gain,
    ln1_bias,
    w_qkv,
    qv_bias,
    w_out,
    out_bias,
    ln2_gain,
    ln2_bias,
    w_up,
    up_bias,
    w_down,
    down_bias,
    d_output,
):
    f32 = jnp.float32
    b16 = jnp.bfloat16
    half_rows = hidden.shape[3]
    width = hidden.shape[4]
    tok_rows = 2 * half_rows
    groups = lax.axis_size("fsdp")
    ctx_size = lax.axis_size("ctx")
    head_count = alibi_slopes.shape[0]
    head_width = width // head_count
    heads = head_count // groups
    span = tok_rows * groups
    block_span = half_rows * groups
    parts = ctx_size // heads
    part_groups = groups // parts
    query_rows = part_groups * half_rows
    half = query_rows // 2
    qkv_cols = 3 * width // groups
    up_cols = w_up.shape[1] // groups
    ctx_index = lax.axis_index("ctx")
    group_index = lax.axis_index("fsdp")
    shard = width // groups
    cut = w_qkv.shape[0] // ctx_size

    def gather(rows, axis_name):
        return lax.all_gather(rows, axis_name, axis=0, tiled=True)

    def exchange(rows, axis_name):
        return lax.all_to_all(rows, axis_name, split_axis=0, concat_axis=0, tiled=True)

    def scatter(rows):
        return lax.psum_scatter(
            rows.astype(b16), "fsdp", scatter_dimension=0, tiled=True
        ).astype(f32)

    def dot_tn(left, right):
        return lax.dot_general(
            left, right, (((0,), (0,)), ((), ())), preferred_element_type=f32
        ).astype(b16)

    def spread(sums):
        sums = sums.reshape(-1, shard).T
        mine = jnp.arange(groups)[:, None, None] == group_index
        return jnp.where(mine, sums[None], 0.0).reshape(width, -1)

    def own_row_sums(cols, extras):
        extra = jnp.concatenate(extras, axis=1)
        extra = jnp.pad(extra, ((0, 0), (0, 128 - extra.shape[1]))).astype(b16)
        total = cols.shape[1]
        cols = jnp.concatenate([cols, extra], axis=1)
        cols = cols.reshape(groups, ctx_size, cut, total + 128).transpose(1, 0, 2, 3)
        terms = exchange(cols, "ctx")
        moved = exchange(jnp.sum(terms.astype(f32), axis=0).astype(b16), "fsdp")
        main = moved[:, :, :total].transpose(1, 0, 2).reshape(cut, groups * total)
        rest = jnp.sum(moved[:, :, total:].astype(f32), axis=0).astype(b16)
        whole = gather(jnp.concatenate([main, rest], axis=1), "ctx").astype(f32)
        return whole[:, : groups * total], whole[:, groups * total :]

    cut_qkv = lax.dynamic_slice_in_dim(w_qkv, ctx_index * cut, cut).reshape(cut, groups, qkv_cols)
    cut_up = lax.dynamic_slice_in_dim(w_up, ctx_index * cut, cut).reshape(cut, groups, up_cols)
    cut_qkv = exchange(cut_qkv.transpose(1, 0, 2), "fsdp")
    cut_qkv, cut_up = lax.optimization_barrier((cut_qkv, cut_up))
    cut_up = exchange(cut_up.transpose(1, 0, 2), "fsdp")

    def own_columns(cut_cols):
        whole = lax.all_gather(cut_cols, "ctx", axis=0)
        return whole.transpose(1, 0, 2, 3).reshape(width, cut_cols.shape[2])

    own_qkv = own_columns(cut_qkv)
    own_up = own_columns(cut_up)

    own_rows = hidden.reshape(tok_rows, width)
    grad_out = d_output.reshape(tok_rows, width)
    small = jnp.stack([ln1_gain, ln1_bias, out_bias, ln2_gain, ln2_bias, down_bias])
    small = jnp.pad(small, ((0, 10), (0, width - shard)))
    with_small = gather(jnp.concatenate([own_rows, small], axis=0), "fsdp").reshape(
        groups, tok_rows + 16, width
    )
    full_small = (
        with_small[:, tok_rows : tok_rows + 6, :shard].transpose(1, 0, 2).reshape(6, width)
    ).astype(f32)
    full_g1, full_b1, full_bo, full_g2, full_b2, full_bd = (full_small[i] for i in range(6))
    all_rows = with_small[:, :tok_rows].reshape(span, width)
    all_grad = gather(grad_out, "fsdp")

    rows_in = own_rows.astype(f32)
    normed_one, inv_one = norm_parts(rows_in)
    normed_all = norm_parts(all_rows.astype(f32))[0]
    first_in = (normed_all * full_g1 + full_b1).astype(b16)
    joined_bias = jnp.concatenate(
        [
            qv_bias[:, :head_width],
            jnp.zeros((heads, head_width), b16),
            qv_bias[:, head_width:],
        ],
        axis=1,
    ).reshape(qkv_cols)
    joined = (dot_nn(first_in, own_qkv) + joined_bias.astype(f32)).astype(b16)

    joined = joined.reshape(parts, part_groups, 2, half_rows, heads, 3 * head_width)

    def pack_queries(rows):
        rows = rows.transpose(4, 0, 2, 1, 3, 5).reshape(
            ctx_size, 2, 2, half, head_width
        )
        return jnp.concatenate([rows[:, :, 0], rows[:, :, 1]], axis=-1)

    def unpack_queries(rows):
        rows = jnp.stack([rows[..., :head_width], rows[..., head_width:]], axis=2)
        return rows.reshape(
            heads, parts, 2, part_groups, half_rows, head_width
        ).transpose(1, 3, 2, 4, 0, 5)

    keys_values = (
        joined[..., head_width:]
        .transpose(4, 2, 0, 1, 3, 5)
        .reshape(heads, 1, 2, block_span, 2 * head_width)
    )
    keys_values = jnp.broadcast_to(
        keys_values, (heads, parts, 2, block_span, 2 * head_width)
    ).reshape(ctx_size, 2, block_span, 2 * head_width)
    packed = exchange(
        jnp.concatenate([keys_values, pack_queries(joined[..., :head_width])], axis=2), "ctx"
    ).reshape(2 * ctx_size, block_span + half, 2 * head_width)

    flat_order = block_order.reshape(-1)
    slot_ids = jnp.arange(2 * ctx_size, dtype=jnp.int32)
    slots = jnp.sum(
        jnp.where(flat_order[None, :] == slot_ids[:, None], slot_ids[None, :], 0), axis=1
    ).astype(jnp.int32)
    part = (ctx_index % parts).astype(jnp.int32).reshape(1)
    slope = lax.dynamic_slice_in_dim(alibi_slopes, group_index * heads + ctx_index // parts, 1)
    out_packed, out_t, lse = attend(slots, part, slope, packed, block_span)
    out_packed, own_up, all_grad = lax.optimization_barrier((out_packed, own_up, all_grad))

    attended = unpack_queries(
        exchange(out_packed.reshape(ctx_size, 2, half, 2 * head_width), "ctx")
    ).reshape(span, heads * head_width)
    middle = rows_in + scatter(dot_nn(attended, w_out)) + full_bo
    normed_two, inv_two = norm_parts(middle)
    second_in = gather((normed_two * full_g2 + full_b2).astype(b16), "fsdp")
    hidden_pre = dot_nn(second_in, own_up) + up_bias.astype(f32)
    activated, gelu_pull = jax.vjp(gelu_tanh, hidden_pre)
    activated = activated.astype(b16)
    grad_act = dot_nt(all_grad, w_down).astype(b16)
    grad_pre = gelu_pull(grad_act.astype(f32))[0].astype(b16)
    grad_second = scatter(dot_nt(grad_pre, own_up))
    grad_middle = grad_out.astype(f32) + norm_back(grad_second, full_g2, normed_two, inv_two)
    own_branch = grad_middle.astype(b16)
    grad_branch = gather(own_branch, "fsdp")
    down_term, grad_branch = lax.optimization_barrier(
        (dot_nn(activated, w_down).astype(b16), grad_branch)
    )
    result = middle + scatter(down_term) + full_bd
    output = result.astype(b16).reshape(hidden.shape)
    grad_attended = dot_nt(grad_branch, w_out).astype(b16)
    grad_packed = exchange(
        pack_queries(
            grad_attended.reshape(parts, part_groups, 2, half_rows, heads, head_width)
        ),
        "ctx",
    ).reshape(2 * ctx_size, half, 2 * head_width)
    grads = attend_back(slots, part, slope, packed, grad_packed, out_t, lse, block_span)
    grads = exchange(
        grads.reshape(ctx_size, 2, block_span + half, 2 * head_width), "ctx"
    )
    d_w_down, d_w_out = lax.psum(
        (dot_tn(activated, all_grad), dot_tn(attended, grad_branch)), "ctx"
    )
    d_w_up, up_sums = own_row_sums(
        dot_tn(second_in, grad_pre),
        [
            jnp.sum(grad_second * normed_two, axis=0)[:, None],
            jnp.sum(grad_second, axis=0)[:, None],
            jnp.sum(own_branch.astype(f32), axis=0)[:, None],
            jnp.sum(grad_out.astype(f32), axis=0)[:, None],
            spread(jnp.sum(grad_pre.astype(f32), axis=0)),
        ],
    )
    grads, d_w_down, d_w_out = lax.optimization_barrier((grads, d_w_down, d_w_out))
    grad_q = unpack_queries(grads[:, :, block_span:]).reshape(span, heads, head_width)
    grad_kv = jnp.sum(
        grads[:, :, :block_span]
        .reshape(heads, parts, 2, groups, half_rows, 2 * head_width)
        .astype(f32),
        axis=1,
    ).astype(b16)
    grad_kv = grad_kv.transpose(2, 1, 3, 0, 4).reshape(span, heads, 2 * head_width)
    grad_joined = jnp.concatenate([grad_q, grad_kv], axis=2).reshape(span, qkv_cols)
    first_term = dot_nt(grad_joined, own_qkv)
    grad_first = scatter(first_term)
    grad_rows = grad_middle + norm_back(grad_first, full_g1, normed_one, inv_one)
    d_hidden = grad_rows.astype(b16).reshape(hidden.shape)

    joined_sums = jnp.sum(grad_joined.astype(f32), axis=0).reshape(heads, 3, head_width)
    sum_qv = jnp.concatenate([joined_sums[:, 0], joined_sums[:, 2]], axis=1)
    d_w_qkv, qkv_sums = own_row_sums(
        dot_tn(first_in, grad_joined),
        [
            jnp.sum(first_term * normed_all, axis=0)[:, None],
            jnp.sum(first_term, axis=0)[:, None],
            spread(sum_qv.reshape(-1)),
        ],
    )
    qv_lanes = sum_qv.size // shard
    d_qv_bias = qkv_sums[:, 2 : 2 + qv_lanes].T.reshape(sum_qv.shape)
    up_lanes = up_cols // shard
    d_up_bias = up_sums[:, 4 : 4 + up_lanes].T.reshape(up_cols)
    return (
        output,
        d_hidden,
        qkv_sums[:, 0],
        qkv_sums[:, 1],
        d_w_qkv,
        d_qv_bias,
        d_w_out.astype(f32),
        up_sums[:, 2],
        up_sums[:, 0],
        up_sums[:, 1],
        d_w_up,
        d_up_bias,
        d_w_down.astype(f32),
        up_sums[:, 3],
    )


def solution(mesh):
    placed = (
        P("ctx", None, "fsdp", None, None),
        P(),
        P(),
        P("fsdp"),
        P("fsdp"),
        P("fsdp", None),
        P("fsdp", None),
        P("fsdp", None),
        P("fsdp"),
        P("fsdp"),
        P("fsdp"),
        P("fsdp", None),
        P("fsdp"),
        P("fsdp", None),
        P("fsdp"),
        P("ctx", None, "fsdp", None, None),
    )
    return jax.shard_map(
        local,
        mesh=mesh,
        in_specs=placed,
        out_specs=(
            P("ctx", None, "fsdp", None, None),
            P("ctx", None, "fsdp", None, None),
            P("fsdp"),
            P("fsdp"),
            P("fsdp", None),
            P("fsdp", None),
            P("fsdp", None),
            P("fsdp"),
            P("fsdp"),
            P("fsdp"),
            P("fsdp", None),
            P("fsdp"),
            P("fsdp", None),
            P("fsdp"),
        ),
        check_vma=False,
    )
```

```python
import functools

import jax
import jax.numpy as jnp
from jax import lax
from jax.experimental import pallas as pl
from jax.experimental.pallas import tpu as pltpu
from jax.sharding import PartitionSpec as P

EPSILON = 1e-05
NEGATIVE = -1e30
TANH_SCALE = 0.7978845608028654


def gelu_tanh(values):
    return (
        0.5 * values * (1.0 + jnp.tanh(TANH_SCALE * (values + 0.044715 * values * values * values)))
    )


def norm_parts(rows_in):
    centred = rows_in - jnp.mean(rows_in, axis=-1, keepdims=True)
    inv_std = lax.rsqrt(jnp.mean(centred * centred, axis=-1, keepdims=True) + EPSILON)
    return (centred * inv_std, inv_std)


def norm_back(d_norm, gain, normed, inv_std):
    scaled = d_norm * gain
    return inv_std * (
        scaled
        - jnp.mean(scaled, axis=-1, keepdims=True)
        - normed * jnp.mean(scaled * normed, axis=-1, keepdims=True)
    )


TILE_BLOCKS = 4


def dot_nt(left, right):
    return lax.dot_general(left, right, (((1,), (1,)), ((), ())), preferred_element_type=jnp.float32)


def dot_nn(left, right):
    return jnp.dot(left, right, preferred_element_type=jnp.float32)


def query_places(tile, part, query_rows, tile_rows, block_span):
    lane = lax.broadcasted_iota(jnp.int32, (1, tile_rows), 1)
    block = tile * TILE_BLOCKS + lane // query_rows
    return (block * block_span + part * query_rows + lane % query_rows).astype(jnp.float32)


def key_places(block, block_span):
    row = lax.broadcasted_iota(jnp.int32, (block_span, 1), 0)
    return (block * block_span + row).astype(jnp.float32)


def sort_rows(slots, source, first, half, width, target, scale):
    blocks = source.shape[0]

    def step(block, carry):
        packed = source[slots[block], pl.ds(first, half), :].astype(jnp.float32) * scale
        base = pl.multiple_of(block * 2 * half, 2 * half)
        target[pl.ds(base, half), :] = packed[:, :width].astype(target.dtype)
        target[pl.ds(base + half, half), :] = packed[:, width:].astype(target.dtype)
        return carry

    lax.fori_loop(0, blocks, step, 0)


def unsort_rows(slots, source, first, half, target):
    blocks = target.shape[0]

    def step(block, carry):
        base = pl.multiple_of(block * 2 * half, 2 * half)
        packed = jnp.concatenate(
            [source[pl.ds(base, half), :], source[pl.ds(base + half, half), :]], axis=1
        )
        target[slots[block], pl.ds(first, half), :] = packed.astype(target.dtype)
        return carry

    lax.fori_loop(0, blocks, step, 0)


def attend_kernel(
    block_span, slots, part, slope, packed, out, out_t, lse, sorted_q, run_max, run_sum, sorted_o
):
    blocks = packed.shape[0]
    half = packed.shape[1] - block_span
    width = packed.shape[2] // 2
    rows = 2 * half
    tile_rows = TILE_BLOCKS * rows
    sort_rows(slots, packed, block_span, half, width, sorted_q, 0.125)
    run_max[...] = jnp.full_like(run_max, NEGATIVE)
    run_sum[...] = jnp.zeros_like(run_sum)
    out_t[...] = jnp.zeros_like(out_t)
    slope_now = slope[0]
    part_now = part[0]

    def key_step(block, carry):
        keys = packed[slots[block], pl.ds(0, block_span), :]
        values_t = keys[:, width:].astype(jnp.float32).T.astype(jnp.bfloat16)
        keys = keys[:, :width]
        key_pos = key_places(block, block_span)

        def tile_step(tile, inner):
            base = pl.multiple_of(tile * tile_rows, tile_rows)
            where = pl.ds(base, tile_rows)
            gap = query_places(tile, part_now, rows, tile_rows, block_span) - key_pos
            score = dot_nt(keys, sorted_q[where, :]) - slope_now * gap
            score = jnp.where(gap >= 0.0, score, NEGATIVE)
            old_max = run_max[:, where]
            new_max = jnp.maximum(old_max, jnp.max(score, axis=0, keepdims=True))
            weights = jnp.exp(score - new_max)
            shrink = jnp.exp(old_max - new_max)
            run_max[:, where] = new_max
            run_sum[:, where] = run_sum[:, where] * shrink + jnp.sum(
                weights, axis=0, keepdims=True
            )
            out_t[:, where] = out_t[:, where] * shrink + dot_nn(
                values_t, weights.astype(jnp.bfloat16)
            )
            return inner

        lax.fori_loop(block // TILE_BLOCKS, blocks // TILE_BLOCKS, tile_step, 0)
        return carry

    lax.fori_loop(0, blocks, key_step, 0)
    out_t[...] = out_t[...] / run_sum[...]
    lse[...] = run_max[...] + jnp.log(run_sum[...])
    sorted_o[...] = out_t[...].T
    unsort_rows(slots, sorted_o, 0, half, out)


def attend_back_kernel(
    block_span,
    slots,
    part,
    slope,
    packed,
    grad_out,
    out_t,
    lse,
    grads,
    sorted_q,
    sorted_g,
    delta,
    grad_q_t,
    sorted_dq,
):
    blocks = packed.shape[0]
    half = packed.shape[1] - block_span
    width = packed.shape[2] // 2
    rows = 2 * half
    tile_rows = TILE_BLOCKS * rows
    sort_rows(slots, packed, block_span, half, width, sorted_q, 0.125)
    sort_rows(slots, grad_out, 0, half, width, sorted_g, 1.0)
    delta[...] = jnp.sum(
        sorted_g[...].astype(jnp.float32).T * out_t[...], axis=0, keepdims=True
    )
    grad_q_t[...] = jnp.zeros_like(grad_q_t)
    slope_now = slope[0]
    part_now = part[0]

    def key_step(block, carry):
        keys = packed[slots[block], pl.ds(0, block_span), :]
        values = keys[:, width:]
        keys = keys[:, :width]
        keys_t = keys.astype(jnp.float32).T.astype(jnp.bfloat16)
        key_pos = key_places(block, block_span)

        def tile_step(tile, sums):
            grad_k, grad_v = sums
            base = pl.multiple_of(tile * tile_rows, tile_rows)
            where = pl.ds(base, tile_rows)
            query_now = sorted_q[where, :]
            grad_now = sorted_g[where, :]
            gap = query_places(tile, part_now, rows, tile_rows, block_span) - key_pos
            score = dot_nt(keys, query_now) - slope_now * gap
            score = jnp.where(gap >= 0.0, score, NEGATIVE)
            probs = jnp.exp(score - lse[:, where])
            grad_v = grad_v + dot_nn(probs.astype(jnp.bfloat16), grad_now)
            grad_score = probs * (dot_nt(values, grad_now) - delta[:, where])
            grad_score = grad_score.astype(jnp.bfloat16)
            grad_k = grad_k + dot_nn(grad_score, query_now)
            grad_q_t[:, where] = grad_q_t[:, where] + dot_nn(keys_t, grad_score)
            return (grad_k, grad_v)

        zero = jnp.zeros((block_span, width), jnp.float32)
        grad_k, grad_v = lax.fori_loop(
            block // TILE_BLOCKS, blocks // TILE_BLOCKS, tile_step, (zero, zero)
        )
        grads[slots[block], pl.ds(0, block_span), :] = jnp.concatenate(
            [grad_k, grad_v], axis=1
        ).astype(grads.dtype)
        return carry

    lax.fori_loop(0, blocks, key_step, 0)
    sorted_dq[...] = grad_q_t[...].T * 0.125
    unsort_rows(slots, sorted_dq, block_span, half, grads)


def smem():
    return pl.BlockSpec(memory_space=pltpu.SMEM)


def vmem():
    return pl.BlockSpec(memory_space=pltpu.VMEM)


def attend(slots, part, slope, packed, block_span):
    blocks, packed_rows, lanes = packed.shape
    half = packed_rows - block_span
    width = lanes // 2
    total = blocks * 2 * half
    return pl.pallas_call(
        functools.partial(attend_kernel, block_span),
        out_shape=(
            jax.ShapeDtypeStruct((blocks, half, lanes), jnp.bfloat16),
            jax.ShapeDtypeStruct((width, total), jnp.float32),
            jax.ShapeDtypeStruct((1, total), jnp.float32),
        ),
        in_specs=[smem(), smem(), smem(), vmem()],
        out_specs=(vmem(), vmem(), vmem()),
        scratch_shapes=[
            pltpu.VMEM((total, width), jnp.bfloat16),
            pltpu.VMEM((1, total), jnp.float32),
            pltpu.VMEM((1, total), jnp.float32),
            pltpu.VMEM((total, width), jnp.float32),
        ],
        compiler_params=pltpu.CompilerParams(vmem_limit_bytes=48 * 1024 * 1024),
        cost_estimate=pl.CostEstimate(
            flops=2 * total * blocks * block_span * lanes,
            bytes_accessed=4 * packed.size,
            transcendentals=total * blocks * block_span // 2,
        ),
        name="attend",
    )(slots, part, slope, packed)


def attend_back(slots, part, slope, packed, grad_out, out_t, lse, block_span):
    blocks, packed_rows, lanes = packed.shape
    half = packed_rows - block_span
    width = lanes // 2
    total = blocks * 2 * half
    return pl.pallas_call(
        functools.partial(attend_back_kernel, block_span),
        out_shape=jax.ShapeDtypeStruct(packed.shape, jnp.bfloat16),
        in_specs=[smem(), smem(), smem(), vmem(), vmem(), vmem(), vmem()],
        out_specs=vmem(),
        scratch_shapes=[
            pltpu.VMEM((total, width), jnp.bfloat16),
            pltpu.VMEM((total, width), jnp.bfloat16),
            pltpu.VMEM((1, total), jnp.float32),
            pltpu.VMEM((width, total), jnp.float32),
            pltpu.VMEM((total, width), jnp.float32),
        ],
        compiler_params=pltpu.CompilerParams(vmem_limit_bytes=48 * 1024 * 1024),
        cost_estimate=pl.CostEstimate(
            flops=5 * total * blocks * block_span * width,
            bytes_accessed=8 * packed.size,
            transcendentals=total * blocks * block_span // 2,
        ),
        name="attend_back",
    )(slots, part, slope, packed, grad_out, out_t, lse)


def local(
    hidden,
    block_order,
    alibi_slopes,
    ln1_gain,
    ln1_bias,
    w_qkv,
    qv_bias,
    w_out,
    out_bias,
    ln2_gain,
    ln2_bias,
    w_up,
    up_bias,
    w_down,
    down_bias,
    d_output,
):
    f32 = jnp.float32
    b16 = jnp.bfloat16
    half_rows = hidden.shape[3]
    width = hidden.shape[4]
    tok_rows = 2 * half_rows
    groups = lax.axis_size("fsdp")
    ctx_size = lax.axis_size("ctx")
    head_count = alibi_slopes.shape[0]
    head_width = width // head_count
    heads = head_count // groups
    span = tok_rows * groups
    block_span = half_rows * groups
    parts = ctx_size // heads
    part_groups = groups // parts
    query_rows = part_groups * half_rows
    half = query_rows // 2
    qkv_cols = 3 * width // groups
    up_cols = w_up.shape[1] // groups
    ctx_index = lax.axis_index("ctx")
    group_index = lax.axis_index("fsdp")
    shard = width // groups
    cut = w_qkv.shape[0] // ctx_size

    def gather(rows, axis_name):
        return lax.all_gather(rows, axis_name, axis=0, tiled=True)

    def exchange(rows, axis_name):
        return lax.all_to_all(rows, axis_name, split_axis=0, concat_axis=0, tiled=True)

    def scatter(rows):
        return lax.psum_scatter(
            rows.astype(b16), "fsdp", scatter_dimension=0, tiled=True
        ).astype(f32)

    def dot_tn(left, right):
        return lax.dot_general(
            left, right, (((0,), (0,)), ((), ())), preferred_element_type=f32
        ).astype(b16)

    def spread(sums):
        sums = sums.reshape(-1, shard).T
        mine = jnp.arange(groups)[:, None, None] == group_index
        return jnp.where(mine, sums[None], 0.0).reshape(width, -1)

    def ctx_terms(cols):
        cols = cols.reshape(groups, ctx_size, cut, cols.shape[1]).transpose(1, 0, 2, 3)
        return exchange(cols, "ctx")

    def to_owners(terms):
        return exchange(jnp.sum(terms.astype(f32), axis=0).astype(b16), "fsdp")

    def own_row_sums(cols, extras, ahead):
        extra = jnp.concatenate(extras, axis=1)
        extra = jnp.pad(extra, ((0, 0), (0, 128 - extra.shape[1]))).astype(b16)
        total = cols.shape[1]
        moved = to_owners(ctx_terms(jnp.concatenate([cols, extra], axis=1)))
        moved, ahead = lax.optimization_barrier((moved, ahead))
        main = moved[:, :, :total].transpose(1, 0, 2).reshape(cut, groups * total)
        rest = jnp.sum(moved[:, :, total:].astype(f32), axis=0).astype(b16)
        whole = gather(jnp.concatenate([main, rest], axis=1), "ctx").astype(f32)
        return whole[:, : groups * total], whole[:, groups * total :], ahead

    cut_qkv = lax.dynamic_slice_in_dim(w_qkv, ctx_index * cut, cut).reshape(cut, groups, qkv_cols)
    cut_up = lax.dynamic_slice_in_dim(w_up, ctx_index * cut, cut).reshape(cut, groups, up_cols)
    cut_qkv = exchange(cut_qkv.transpose(1, 0, 2), "fsdp")
    cut_qkv, cut_up = lax.optimization_barrier((cut_qkv, cut_up))
    cut_up = exchange(cut_up.transpose(1, 0, 2), "fsdp")

    def own_columns(cut_cols):
        whole = lax.all_gather(cut_cols, "ctx", axis=0)
        return whole.transpose(1, 0, 2, 3).reshape(width, cut_cols.shape[2])

    own_qkv = own_columns(cut_qkv)
    own_up = own_columns(cut_up)

    own_rows = hidden.reshape(tok_rows, width)
    grad_out = d_output.reshape(tok_rows, width)
    small = jnp.stack([ln1_gain, ln1_bias, out_bias, ln2_gain, ln2_bias, down_bias])
    small = jnp.pad(small, ((0, 10), (0, width - shard)))
    with_small = gather(jnp.concatenate([own_rows, small], axis=0), "fsdp").reshape(
        groups, tok_rows + 16, width
    )
    full_small = (
        with_small[:, tok_rows : tok_rows + 6, :shard].transpose(1, 0, 2).reshape(6, width)
    ).astype(f32)
    full_g1, full_b1, full_bo, full_g2, full_b2, full_bd = (full_small[i] for i in range(6))
    all_rows = with_small[:, :tok_rows].reshape(span, width)
    all_grad = gather(grad_out, "fsdp")

    rows_in = own_rows.astype(f32)
    normed_one, inv_one = norm_parts(rows_in)
    normed_all = norm_parts(all_rows.astype(f32))[0]
    first_in = (normed_all * full_g1 + full_b1).astype(b16)
    joined_bias = jnp.concatenate(
        [
            qv_bias[:, :head_width],
            jnp.zeros((heads, head_width), b16),
            qv_bias[:, head_width:],
        ],
        axis=1,
    ).reshape(qkv_cols)
    joined = (dot_nn(first_in, own_qkv) + joined_bias.astype(f32)).astype(b16)

    joined = joined.reshape(parts, part_groups, 2, half_rows, heads, 3 * head_width)

    def pack_queries(rows):
        rows = rows.transpose(4, 0, 2, 1, 3, 5).reshape(
            ctx_size, 2, 2, half, head_width
        )
        return jnp.concatenate([rows[:, :, 0], rows[:, :, 1]], axis=-1)

    def unpack_queries(rows):
        rows = jnp.stack([rows[..., :head_width], rows[..., head_width:]], axis=2)
        return rows.reshape(
            heads, parts, 2, part_groups, half_rows, head_width
        ).transpose(1, 3, 2, 4, 0, 5)

    keys_values = (
        joined[..., head_width:]
        .transpose(4, 2, 0, 1, 3, 5)
        .reshape(heads, 1, 2, block_span, 2 * head_width)
    )
    keys_values = jnp.broadcast_to(
        keys_values, (heads, parts, 2, block_span, 2 * head_width)
    ).reshape(ctx_size, 2, block_span, 2 * head_width)
    packed = exchange(
        jnp.concatenate([keys_values, pack_queries(joined[..., :head_width])], axis=2), "ctx"
    ).reshape(2 * ctx_size, block_span + half, 2 * head_width)

    flat_order = block_order.reshape(-1)
    slot_ids = jnp.arange(2 * ctx_size, dtype=jnp.int32)
    slots = jnp.sum(
        jnp.where(flat_order[None, :] == slot_ids[:, None], slot_ids[None, :], 0), axis=1
    ).astype(jnp.int32)
    part = (ctx_index % parts).astype(jnp.int32).reshape(1)
    slope = lax.dynamic_slice_in_dim(alibi_slopes, group_index * heads + ctx_index // parts, 1)
    out_packed, out_t, lse = attend(slots, part, slope, packed, block_span)
    out_packed, own_up, all_grad = lax.optimization_barrier((out_packed, own_up, all_grad))

    attended = unpack_queries(
        exchange(out_packed.reshape(ctx_size, 2, half, 2 * head_width), "ctx")
    ).reshape(span, heads * head_width)
    middle = rows_in + scatter(dot_nn(attended, w_out)) + full_bo
    normed_two, inv_two = norm_parts(middle)
    second_in = gather((normed_two * full_g2 + full_b2).astype(b16), "fsdp")
    hidden_pre = dot_nn(second_in, own_up) + up_bias.astype(f32)
    activated, gelu_pull = jax.vjp(gelu_tanh, hidden_pre)
    activated = activated.astype(b16)
    grad_act = dot_nt(all_grad, w_down).astype(b16)
    grad_pre = gelu_pull(grad_act.astype(f32))[0].astype(b16)
    down_terms = exchange(dot_tn(activated, all_grad).reshape(ctx_size, -1, width), "ctx")
    grad_second = scatter(dot_nt(grad_pre, own_up))
    grad_second, down_terms = lax.optimization_barrier((grad_second, down_terms))
    up_terms = ctx_terms(dot_tn(second_in, grad_pre))
    grad_middle = grad_out.astype(f32) + norm_back(grad_second, full_g2, normed_two, inv_two)
    own_branch = grad_middle.astype(b16)
    grad_branch = gather(own_branch, "fsdp")
    down_sum = jnp.sum(down_terms.astype(f32), axis=0).astype(b16)
    down_term, grad_branch, up_terms, down_sum = lax.optimization_barrier(
        (dot_nn(activated, w_down).astype(b16), grad_branch, up_terms, down_sum)
    )
    d_w_out = lax.psum(dot_tn(attended, grad_branch), "ctx")
    d_w_down = gather(down_sum, "ctx")
    moved_up = to_owners(up_terms)
    down_added = scatter(down_term)
    grad_attended = dot_nt(grad_branch, w_out).astype(b16)
    grad_packed = exchange(
        pack_queries(
            grad_attended.reshape(parts, part_groups, 2, half_rows, heads, head_width)
        ),
        "ctx",
    ).reshape(2 * ctx_size, half, 2 * head_width)
    grads = attend_back(slots, part, slope, packed, grad_packed, out_t, lse, block_span)
    grads, moved_up = lax.optimization_barrier((grads, moved_up))
    d_w_up = gather(moved_up.transpose(1, 0, 2).reshape(cut, groups * up_cols), "ctx")
    grads = exchange(
        grads.reshape(ctx_size, 2, block_span + half, 2 * head_width), "ctx"
    )
    grads, d_w_down, d_w_out = lax.optimization_barrier((grads, d_w_down, d_w_out))
    grad_q = unpack_queries(grads[:, :, block_span:]).reshape(span, heads, head_width)
    grad_kv = jnp.sum(
        grads[:, :, :block_span]
        .reshape(heads, parts, 2, groups, half_rows, 2 * head_width)
        .astype(f32),
        axis=1,
    ).astype(b16)
    grad_kv = grad_kv.transpose(2, 1, 3, 0, 4).reshape(span, heads, 2 * head_width)
    grad_joined = jnp.concatenate([grad_q, grad_kv], axis=2).reshape(span, qkv_cols)
    first_term = dot_nt(grad_joined, own_qkv)
    grad_first = scatter(first_term)
    grad_rows = grad_middle + norm_back(grad_first, full_g1, normed_one, inv_one)
    d_hidden = grad_rows.astype(b16).reshape(hidden.shape)

    joined_sums = jnp.sum(grad_joined.astype(f32), axis=0).reshape(heads, 3, head_width)
    sum_qv = jnp.concatenate([joined_sums[:, 0], joined_sums[:, 2]], axis=1)
    d_w_qkv, qkv_sums, (d_w_up, down_added) = own_row_sums(
        dot_tn(first_in, grad_joined),
        [
            jnp.sum(first_term * normed_all, axis=0)[:, None],
            jnp.sum(first_term, axis=0)[:, None],
            jnp.sum(grad_second * normed_two, axis=0)[:, None],
            jnp.sum(grad_second, axis=0)[:, None],
            jnp.sum(own_branch.astype(f32), axis=0)[:, None],
            jnp.sum(grad_out.astype(f32), axis=0)[:, None],
            spread(jnp.sum(grad_pre.astype(f32), axis=0)),
            spread(sum_qv.reshape(-1)),
        ],
        (d_w_up, down_added),
    )
    sums = qkv_sums[:, :32].T
    output = (middle + down_added + full_bd).astype(b16).reshape(hidden.shape)
    qv_lanes = sum_qv.size // shard
    up_lanes = up_cols // shard
    d_up_bias = sums[6 : 6 + up_lanes].reshape(up_cols)
    d_qv_bias = sums[6 + up_lanes : 6 + up_lanes + qv_lanes].reshape(sum_qv.shape)
    return (
        output,
        d_hidden,
        sums[0],
        sums[1],
        d_w_qkv,
        d_qv_bias,
        d_w_out.astype(f32),
        sums[4],
        sums[2],
        sums[3],
        d_w_up.astype(f32),
        d_up_bias,
        d_w_down.astype(f32),
        sums[5],
    )


def solution(mesh):
    placed = (
        P("ctx", None, "fsdp", None, None),
        P(),
        P(),
        P("fsdp"),
        P("fsdp"),
        P("fsdp", None),
        P("fsdp", None),
        P("fsdp", None),
        P("fsdp"),
        P("fsdp"),
        P("fsdp"),
        P("fsdp", None),
        P("fsdp"),
        P("fsdp", None),
        P("fsdp"),
        P("ctx", None, "fsdp", None, None),
    )
    return jax.shard_map(
        local,
        mesh=mesh,
        in_specs=placed,
        out_specs=(
            P("ctx", None, "fsdp", None, None),
            P("ctx", None, "fsdp", None, None),
            P("fsdp"),
            P("fsdp"),
            P("fsdp", None),
            P("fsdp", None),
            P("fsdp", None),
            P("fsdp"),
            P("fsdp"),
            P("fsdp"),
            P("fsdp", None),
            P("fsdp"),
            P("fsdp", None),
            P("fsdp"),
        ),
        check_vma=False,
    )
```
